32 devices in a mesh: dev: 32 (over z, y, x, core).
Axes of the slice: x: 2, y: 2, z: 4, core: 2. Of those that a mesh axis runs over, the one named last changes fastest.
Arguments:
- start: float32 [8, 65536], P(None, 'dev'), may hold values from -18 to 18
- self_blocks: bfloat16 [256, 256, 256], P('dev'), may hold values from -1 to 5, as said below
- near_pairs: int32 [2, 3072], P(None, 'dev'), may hold values from 0 to 255, as said below
- near_blocks: bfloat16 [3072, 256, 256], P('dev'), may hold values from -0.08984375 to 0.08984375
- far_pairs: int32 [2, 4096], P(None, 'dev'), may hold values from 0 to 255, as said below
- far_left: bfloat16 [4096, 16, 256], P('dev'), may hold values from -0.375 to 0.375
- far_right: bfloat16 [4096, 16, 256], P('dev'), may hold values from -0.375 to 0.375
Outputs:
- next_basis: float32 [8, 65536], P(None, 'dev')
- hessenberg: float32 [5, 8], replicated
The draws below stay inside these ranges and needn't reach their ends.
Inputs may be any that keep to these rules, and one draw needn't show every extreme that they name: `self_blocks`: each block equals its transpose. `near_pairs`: the first cluster of a pair lies on the owning device; the second differs from it and lies on the owning device or on the device just before or after it. `far_pairs`: the first cluster of a pair lies on the owning device; the second lies on another device; among one device's 128 pairs at most 8 have their second cluster on any one device, and exactly 8 on the next device and on the device half the axis away.
All inputs are finite; a program needn't handle non-finite values.
Results may differ from the reference program's by a relative error of at most 0.009.
Values may be sent and summed in bfloat16 or wider, within the bound.
A program may use at most 128 MiB of HBM per device.

```python
import math
import jax
import jax.numpy as jnp
from jax import lax

PAN = 256
RANK = 16
RHS = 8
CL_DEV = 8
NEAR_DEV = 96
FAR_DEV = 128
MOST = 8
CLUSTERS = 256
PANELS = 65536
N_DEV = 32


def draw_start(key, part):
    key = jax.random.fold_in(key, 7)
    first = jax.random.fold_in(key, 0)
    place = jnp.arange(PANELS, dtype=jnp.float32) / float(PANELS)
    ramp = jnp.exp(math.log(3.0) * place)[None, :]
    values = jnp.clip(jax.random.normal(first, (RHS, PANELS), jnp.float32), -6.0, 6.0) * ramp
    return jnp.clip(values, -18.0, 18.0).astype(jnp.float32)


def draw_self_blocks(key, part):
    key = jax.random.fold_in(key, 5)
    first, second = jax.random.split(key)
    noise = jnp.clip(jax.random.normal(first, (CLUSTERS, PAN, PAN), jnp.float32), -6.0, 6.0)
    mirrored = (noise + jnp.swapaxes(noise, 1, 2)) * (0.28 / math.sqrt(PAN))
    diagonal = jnp.exp(jax.random.uniform(second, (CLUSTERS, PAN), jnp.float32, 0.0, math.log(4.0)))
    identity = jnp.eye(PAN, dtype=jnp.float32)
    return (mirrored + diagonal[:, :, None] * identity[None, :, :]).astype(jnp.bfloat16)


def draw_near_pairs(key, part):
    key = jax.random.fold_in(key, 11)
    first, second, third, fourth = jax.random.split(key, 4)
    total = NEAR_DEV * N_DEV
    owner = jnp.arange(total, dtype=jnp.int32) // NEAR_DEV
    row_local = jax.random.randint(first, (total,), 0, CL_DEV)
    offset = jax.random.randint(second, (total,), -1, 2)
    offset = jnp.where(owner + offset < 0, 0, offset)
    offset = jnp.where(owner + offset >= N_DEV, 0, offset)
    col_any = jax.random.randint(third, (total,), 0, CL_DEV)
    col_same = (row_local + 1 + jax.random.randint(fourth, (total,), 0, CL_DEV - 1)) % CL_DEV
    col_local = jnp.where(offset == 0, col_same, col_any)
    rows = owner * CL_DEV + row_local
    cols = (owner + offset) * CL_DEV + col_local
    return jnp.stack([rows, cols]).astype(jnp.int32)


def draw_far_pairs(key, part):
    key = jax.random.fold_in(key, 23)
    first, second, third, fourth = jax.random.split(key, 4)
    slots = N_DEV * MOST
    owner = jnp.arange(N_DEV, dtype=jnp.int32)[:, None]
    slot_target = (jnp.arange(slots, dtype=jnp.int32) // MOST)[None, :]
    noise = jax.random.randint(first, (N_DEV, slots), 0, 4096) * slots + jnp.arange(slots, dtype=jnp.int32)[None, :]
    limit = 4096 * slots
    banned = slot_target == owner
    forced = (slot_target == (owner + N_DEV // 2) % N_DEV) | (slot_target == (owner + 1) % N_DEV)
    score = noise + jnp.where(banned, 2 * limit, 0) - jnp.where(forced, 2 * limit, 0)
    chosen = jnp.argsort(score, axis=1, stable=True)[:, :FAR_DEV]
    mixing = jax.random.randint(fourth, (N_DEV, FAR_DEV), 0, 4096) * FAR_DEV + jnp.arange(FAR_DEV, dtype=jnp.int32)[None, :]
    shuffled = jnp.take_along_axis(chosen, jnp.argsort(mixing, axis=1, stable=True), axis=1)
    target = shuffled // MOST
    rows = owner * CL_DEV + jax.random.randint(second, (N_DEV, FAR_DEV), 0, CL_DEV)
    cols = target * CL_DEV + jax.random.randint(third, (N_DEV, FAR_DEV), 0, CL_DEV)
    return jnp.stack([rows.reshape(-1), cols.reshape(-1)]).astype(jnp.int32)


def block_scale(rng, shape, cuts, smallest, top_value):
    level = 1.0
    for dim, parts in cuts:
        heights = jax.random.uniform(jax.random.fold_in(jax.random.fold_in(rng, 6), dim), (parts,), jnp.float32, smallest / len(cuts), top_value / len(cuts))
        level = level * jnp.repeat(jnp.exp(heights), shape[dim] // parts).reshape((-1,) + (1,) * (len(shape) - 1 - dim))
    return level


def scatter_about(own_key, extent, scale, reach, shards=(), kind=jnp.bfloat16):
    loudness = block_scale(own_key, extent, shards, -0.22, 0.18) if shards else 1.0
    values = jax.random.normal(own_key, extent, jnp.float32) * scale * loudness
    return jnp.minimum(jnp.maximum(values, -reach), reach).astype(kind)


def setup_inputs(seed: int = 0) -> dict:
    keys = jax.random.split(jax.random.key(seed), 8)
    start = draw_start(jax.random.fold_in(keys[7], 71), 0)
    self_blocks = draw_self_blocks(jax.random.fold_in(keys[7], 71), 0)
    near_pairs = draw_near_pairs(jax.random.fold_in(keys[7], 71), 0)
    near_blocks = scatter_about(keys[3], (NEAR_DEV * N_DEV, PAN, PAN), 0.015, 0.08984375, ((0, 32),))
    far_pairs = draw_far_pairs(jax.random.fold_in(keys[7], 71), 0)
    far_left = scatter_about(keys[5], (FAR_DEV * N_DEV, RANK, PAN), PAN ** -0.5, 0.375, ((0, 32),))
    far_right = scatter_about(keys[6], (FAR_DEV * N_DEV, RANK, PAN), PAN ** -0.5, 0.375, ((0, 32),))
    return dict(start=start, self_blocks=self_blocks, near_pairs=near_pairs, near_blocks=near_blocks, far_pairs=far_pairs, far_left=far_left, far_right=far_right)


epsilon = 1e-06

def round_bf16(value):
    narrow = lax.optimization_barrier(value.astype(jnp.bfloat16))
    return narrow.astype(jnp.float32)

def apply_operator(vector, self_blocks, near_pairs, near_blocks, far_pairs, far_left, far_right):
    narrow = vector.astype(jnp.bfloat16).astype(jnp.float32)
    clusters = narrow.reshape(RHS, CLUSTERS, PAN).transpose(1, 0, 2)
    grouped = clusters.reshape(N_DEV, CL_DEV, RHS, PAN)
    self_grouped = self_blocks.reshape(N_DEV, CL_DEV, PAN, PAN)

    def self_part(pieces):
        return jnp.einsum('crb,cab->cra', pieces[0], pieces[1].astype(jnp.float32))
    result = lax.map(self_part, (grouped, self_grouped)).reshape(CLUSTERS, RHS, PAN)
    near_rows = near_pairs[0].reshape(N_DEV, NEAR_DEV).astype(jnp.int32)
    near_cols = near_pairs[1].reshape(N_DEV, NEAR_DEV).astype(jnp.int32)
    near_grouped = near_blocks.reshape(N_DEV, NEAR_DEV, PAN, PAN)

    def near_step(total, pieces):
        rows, cols, blocks = pieces
        blocks = blocks.astype(jnp.float32)
        to_rows = jnp.einsum('prb,pab->pra', clusters[cols], blocks)
        to_cols = jnp.einsum('pra,pab->prb', clusters[rows], blocks)
        total = total.at[rows].add(to_rows)
        total = total.at[cols].add(to_cols)
        return (total, None)
    result, _ = lax.scan(near_step, result, (near_rows, near_cols, near_grouped))
    far_rows = far_pairs[0].reshape(N_DEV, FAR_DEV).astype(jnp.int32)
    far_cols = far_pairs[1].reshape(N_DEV, FAR_DEV).astype(jnp.int32)
    left_grouped = far_left.reshape(N_DEV, FAR_DEV, RANK, PAN)
    right_grouped = far_right.reshape(N_DEV, FAR_DEV, RANK, PAN)

    def far_step(total, pieces):
        rows, cols, lefts, rights = pieces
        lefts = lefts.astype(jnp.float32)
        rights = rights.astype(jnp.float32)
        coeff = round_bf16(jnp.einsum('pkb,prb->pkr', rights, clusters[cols]))
        lean = round_bf16(jnp.einsum('pka,pra->pkr', lefts, clusters[rows]))
        total = total.at[rows].add(jnp.einsum('pka,pkr->pra', lefts, coeff))
        total = total.at[cols].add(jnp.einsum('pkb,pkr->prb', rights, lean))
        return (total, None)
    result, _ = lax.scan(far_step, result, (far_rows, far_cols, left_grouped, right_grouped))
    return result.transpose(1, 0, 2).reshape(RHS, PANELS)

def reference(start, self_blocks, near_pairs, near_blocks, far_pairs, far_left, far_right):
    count = float(PANELS)
    scale = jnp.sqrt(lax.optimization_barrier(jnp.sum(start * start, axis=1)) / count + epsilon)
    basis_one = start / scale[:, None]
    image = apply_operator(basis_one, self_blocks, near_pairs, near_blocks, far_pairs, far_left, far_right)
    h_one_one = lax.optimization_barrier(jnp.sum(basis_one * image, axis=1)) / count
    remainder = image - h_one_one[:, None] * basis_one
    h_two_one = jnp.sqrt(lax.optimization_barrier(jnp.sum(remainder * remainder, axis=1)) / count + epsilon)
    basis_two = remainder / h_two_one[:, None]
    image = apply_operator(basis_two, self_blocks, near_pairs, near_blocks, far_pairs, far_left, far_right)
    h_one_two = lax.optimization_barrier(jnp.sum(basis_one * image, axis=1)) / count
    h_two_two = lax.optimization_barrier(jnp.sum(basis_two * image, axis=1)) / count
    remainder = image - h_one_two[:, None] * basis_one - h_two_two[:, None] * basis_two
    h_three_two = jnp.sqrt(lax.optimization_barrier(jnp.sum(remainder * remainder, axis=1)) / count + epsilon)
    next_basis = remainder / h_three_two[:, None]
    hessenberg = jnp.stack([h_one_one, h_two_one, h_one_two, h_two_two, h_three_two])
    return (next_basis, hessenberg)
```

```python
import functools
import jax
import jax.numpy as jnp
from jax import lax
from jax.experimental import pallas as pl
from jax.experimental.pallas import tpu as pltpu
from jax.sharding import PartitionSpec as P

epsilon = 1e-06
LANES = 128
MESH = pl.DeviceIdType.MESH
F32 = jnp.float32
BF16 = jnp.bfloat16
NEAR_CHUNKS = 4
REDUCTIONS = 5


def dot_nn(a, b):
    return lax.dot_general(a, b, (((1,), (0,)), ((), ())), preferred_element_type=F32)


def dot_nt(a, b):
    return lax.dot_general(a, b, (((1,), (1,)), ((), ())), preferred_element_type=F32)


def row_sum(a):
    return jnp.sum(jnp.sum(a, axis=0), axis=1, keepdims=True)


def one_hot_sum(keys, terms, groups):
    count = terms.shape[0]
    hot = jnp.where(lax.broadcasted_iota(jnp.int32, (groups, count), 0) == keys, 1.0, 0.0).astype(BF16)
    high = terms.astype(BF16)
    low = (terms - high.astype(F32)).astype(BF16)
    return dot_nn(hot, high) + dot_nn(hot, low)


def kernel(
    n, most, total_count,
    near_ids, perm, start_ref, keys_ref, row_ids, col_ids, self_hbm, near_hbm, left_hbm, right_hbm,
    out_ref, hess_ref,
    selfs, nears, lefts, rights, factors, outgoing, id_recv, stat_send, stat_recv,
    halo_send, halo_recv, part_send, part_recv, message, message_recv,
    extended, terms, basis,
    load_sem, stat_ssem, stat_rsem, fact_ssem, fact_rsem, id_ssem, id_rsem,
    halo_ssem, halo_rsem, part_ssem, part_rsem, msg_ssem, msg_rsem,
):
    me = lax.axis_index("dev")
    after = lax.rem(me + 1, n)
    before = lax.rem(me + n - 1, n)
    clusters, panels, _ = self_hbm.shape
    pairs = near_hbm.shape[0]
    rank = left_hbm.shape[1]
    rhs = start_ref.shape[0]
    used = most * rank
    flat = clusters * rhs

    def peer_loop(body):
        def step(i, carry):
            body(lax.rem(me + i, n))
            return carry
        lax.fori_loop(1, n, step, 0)

    def remote(src, dst, ssem, rsem, peer):
        return pltpu.make_async_remote_copy(
            src_ref=src, dst_ref=dst, send_sem=ssem, recv_sem=rsem,
            device_id=(peer,), device_id_type=MESH,
        )

    def wait_bytes(ref, sem):
        pltpu.make_async_copy(ref, ref, sem).wait()

    right_copy = pltpu.make_async_copy(right_hbm, rights, load_sem.at[0])
    right_copy.start()
    left_copy = pltpu.make_async_copy(left_hbm, lefts, load_sem.at[1])
    left_copy.start()
    loads = [pltpu.make_async_copy(self_hbm, selfs, load_sem.at[2])]
    size = pairs // NEAR_CHUNKS
    for part in range(NEAR_CHUNKS):
        span = pl.ds(part * size, size)
        loads.append(pltpu.make_async_copy(near_hbm.at[span], nears.at[span], load_sem.at[3 + part]))
    for load in loads:
        load.start()

    barrier = pltpu.get_barrier_semaphore()
    peer_loop(lambda peer: pl.semaphore_signal(barrier, inc=1, device_id=(peer,), device_id_type=MESH))

    lane = lax.broadcasted_iota(jnp.int32, (rhs, LANES), 1)

    def send_stats(index, values):
        block = jnp.zeros((rhs, LANES), F32)
        for place, value in enumerate(values):
            block = jnp.where(lane == place, value, block)
        stat_send[index] = block
        stat_recv[index, me] = block
        peer_loop(lambda peer: remote(
            stat_send.at[index], stat_recv.at[index, me], stat_ssem.at[index], stat_rsem.at[index], peer
        ).start())

    def get_stats(index, count):
        wait_bytes(stat_recv.at[index, pl.ds(0, n - 1)], stat_rsem.at[index])
        total = jnp.sum(stat_recv[index], axis=0)
        return [
            jnp.sum(jnp.where(lane == place, total, 0.0), axis=1, keepdims=True) / total_count
            for place in range(count)
        ]

    first = jnp.stack([start_ref[:, c * panels:(c + 1) * panels] for c in range(clusters)], axis=0)
    partial = row_sum(first * first)

    id_recv[me] = jnp.full((rhs, LANES), -1, jnp.int32)
    if used < LANES:
        def clear(t, carry):
            factors[t] = jnp.zeros((2 * LANES, panels), BF16)
            return carry
        lax.fori_loop(0, n, clear, 0)
    else:
        factors[me] = jnp.zeros((2 * LANES, panels), BF16)
    for it in range(2):
        message_recv[it, me] = jnp.zeros((2 * rhs, LANES), BF16)

    pl.semaphore_wait(barrier, n - 1)
    send_stats(0, [partial])

    right_copy.wait()
    left_copy.wait()

    def send_factors(peer):
        for m in range(most):
            pair = perm[peer * most + m]
            outgoing[peer, pl.ds(m * rank, rank)] = rights[pair]
        remote(col_ids.at[peer], id_recv.at[me], id_ssem.at[0], id_rsem.at[0], peer).start()
        remote(
            outgoing.at[peer], factors.at[me, pl.ds(0, used)], fact_ssem.at[0], fact_rsem.at[0], peer
        ).start()
        for m in range(most):
            pair = perm[peer * most + m]
            factors[peer, pl.ds(LANES + m * rank, rank)] = lefts[pair]

    peer_loop(send_factors)

    (square,) = get_stats(0, 1)
    scale = jnp.sqrt(square + epsilon)
    basis[0] = first / scale[None]

    for load in loads:
        load.wait()

    heights = []
    for it in range(2):
        vector = basis[it].reshape(flat, panels).astype(BF16)
        halo_send[it] = vector
        halos = [
            remote(halo_send.at[it], halo_recv.at[it, 0], halo_ssem.at[it, 0], halo_rsem.at[it, 0], after),
            remote(halo_send.at[it], halo_recv.at[it, 1], halo_ssem.at[it, 1], halo_rsem.at[it, 1], before),
        ]
        for halo in halos:
            halo.start()
        extended[pl.ds(clusters, clusters)] = vector.astype(F32).reshape(clusters, rhs, panels)

        def exchange_far():
            if it == 0:
                wait_bytes(factors.at[pl.ds(0, n - 1), pl.ds(0, used)], fact_rsem.at[0])
                wait_bytes(id_recv.at[pl.ds(0, n - 1)], id_rsem.at[0])

            def products(t4, carry):
                for u in range(4):
                    t = t4 * 4 + u
                    e = dot_nt(vector, factors[t])
                    coeff = jnp.zeros((rhs, LANES), F32)
                    lean = jnp.zeros((rhs, LANES), F32)
                    for c in range(clusters):
                        rows = slice(c * rhs, (c + 1) * rhs)
                        coeff = jnp.where(id_recv[t] == c, e[rows, :LANES], coeff)
                        lean = jnp.where(row_ids[t] == c, e[rows, LANES:], lean)
                    message[it, t] = jnp.concatenate([coeff, lean], axis=0).astype(BF16)
                return carry

            lax.fori_loop(0, n // 4, products, 0)
            peer_loop(lambda peer: remote(
                message.at[it, peer], message_recv.at[it, me], msg_ssem.at[it], msg_rsem.at[it], peer
            ).start())

        if it == 1:
            exchange_far()

        def to_cols(p8, carry):
            for u in range(8):
                p = p8 * 8 + u
                x = extended[near_ids[0, p] + clusters].astype(BF16)
                terms[p] = dot_nn(x, nears[p])
            return carry

        lax.fori_loop(0, pairs // 8, to_cols, 0)
        sums = one_hot_sum(keys_ref[1:2, :], terms[...].reshape(pairs * rhs, panels), 3 * flat)
        part_send[it, 0] = sums[:flat].astype(BF16)
        part_send[it, 1] = sums[2 * flat:].astype(BF16)
        shares = [
            remote(part_send.at[it, 0], part_recv.at[it, 0], part_ssem.at[it, 0], part_rsem.at[it, 0], before),
            remote(part_send.at[it, 1], part_recv.at[it, 1], part_ssem.at[it, 1], part_rsem.at[it, 1], after),
        ]
        for share in shares:
            share.start()
        image = sums[flat:2 * flat]
        image = image + jnp.concatenate(
            [dot_nt(vector[c * rhs:(c + 1) * rhs], selfs[c]) for c in range(clusters)], axis=0
        )
        for halo in halos:
            halo.wait_recv()
        extended[pl.ds(0, clusters)] = halo_recv[it, 0].astype(F32).reshape(clusters, rhs, panels)
        extended[pl.ds(2 * clusters, clusters)] = halo_recv[it, 1].astype(F32).reshape(
            clusters, rhs, panels
        )

        def to_rows(p8, carry):
            for u in range(8):
                p = p8 * 8 + u
                x = extended[near_ids[1, p]].astype(BF16)
                terms[p] = dot_nt(x, nears[p])
            return carry

        lax.fori_loop(0, pairs // 8, to_rows, 0)
        image = image + one_hot_sum(keys_ref[0:1, :], terms[...].reshape(pairs * rhs, panels), flat)
        if it == 0:
            exchange_far()
        for share in shares:
            share.wait_recv()
        has_before = jnp.where(me > 0, 1.0, 0.0)
        has_after = jnp.where(me < n - 1, 1.0, 0.0)
        image = image + part_recv[it, 0].astype(F32) * has_after + part_recv[it, 1].astype(F32) * has_before
        wait_bytes(message_recv.at[it, pl.ds(0, n - 1)], msg_rsem.at[it])

        def far_terms(t4, total):
            for u in range(4):
                t = t4 * 4 + u
                arrived = message_recv[it, t].astype(F32)
                coeff, lean = arrived[:rhs], arrived[rhs:]
                spread = jnp.concatenate(
                    [
                        jnp.concatenate(
                            [
                                jnp.where(id_recv[t] == c, lean, 0.0),
                                jnp.where(row_ids[t] == c, coeff, 0.0),
                            ],
                            axis=1,
                        )
                        for c in range(clusters)
                    ],
                    axis=0,
                ).astype(BF16)
                total = total + dot_nn(spread, factors[t])
            return total

        image = lax.fori_loop(0, n // 4, far_terms, image).reshape(clusters, rhs, panels)

        send_stats(1 + 2 * it, [row_sum(basis[b] * image) for b in range(it + 1)])
        inner = get_stats(1 + 2 * it, it + 1)
        rest = image
        for b in range(it + 1):
            rest = rest - inner[b][None] * basis[b]
        send_stats(2 + 2 * it, [row_sum(rest * rest)])
        (square,) = get_stats(2 + 2 * it, 1)
        norm = jnp.sqrt(square + epsilon)
        heights.extend(inner)
        heights.append(norm)
        following = rest / norm[None]
        if it == 0:
            basis[1] = following
        else:
            for c in range(clusters):
                out_ref[:, c * panels:(c + 1) * panels] = following[c]

    eye = lax.broadcasted_iota(jnp.int32, (rhs, rhs), 0) == lax.broadcasted_iota(jnp.int32, (rhs, rhs), 1)
    for place, height in enumerate(heights):
        hess_ref[place:place + 1, :] = jnp.sum(jnp.where(eye, height, 0.0), axis=0, keepdims=True)

    for index in range(REDUCTIONS):
        wait_bytes(stat_recv.at[index, pl.ds(0, n - 1)], stat_ssem.at[index])
    wait_bytes(factors.at[pl.ds(0, n - 1), pl.ds(0, used)], fact_ssem.at[0])
    wait_bytes(id_recv.at[pl.ds(0, n - 1)], id_ssem.at[0])
    for it in range(2):
        for side in range(2):
            wait_bytes(halo_send.at[it], halo_ssem.at[it, side])
            wait_bytes(part_send.at[it, side], part_ssem.at[it, side])
        wait_bytes(message_recv.at[it, pl.ds(0, n - 1)], msg_ssem.at[it])


def per_device(start, self_blocks, near_pairs, near_blocks, far_pairs, far_left, far_right):
    n = lax.axis_size("dev")
    me = lax.axis_index("dev")
    rhs, width = start.shape
    clusters, panels, _ = self_blocks.shape
    pairs = near_pairs.shape[1]
    far_count = far_pairs.shape[1]
    rank = far_left.shape[1]
    most = max(2, 2 * far_count // n)
    used = most * rank
    flat = clusters * rhs
    near_rows = near_pairs[0] - me * clusters
    near_cols = near_pairs[1] - (me - 1) * clusters
    near_ids = jnp.stack([near_rows, near_cols])
    keys = (near_ids[:, :, None] * rhs + jnp.arange(rhs, dtype=jnp.int32)).reshape(2, pairs * rhs)
    target = far_pairs[1] // clusters
    order = jnp.arange(far_count, dtype=jnp.int32)
    earlier = (target[:, None] == target[None, :]) & (order[None, :] < order[:, None])
    slot = target * most + jnp.sum(earlier.astype(jnp.int32), axis=1)
    hit = slot[None, :] == jnp.arange(n * most, dtype=jnp.int32)[:, None]
    code = order * (clusters * clusters) + (far_pairs[0] - me * clusters) * clusters + far_pairs[1] % clusters
    code = jnp.sum(jnp.where(hit, code[None, :] + 1, 0), axis=1) - 1
    filled = code >= 0
    perm = jnp.where(filled, code // (clusters * clusters), 0)

    def spread(ids):
        ids = jnp.where(filled, ids, -1).reshape(n, most, 1)
        ids = jnp.broadcast_to(ids, (n, most, rank)).reshape(n, 1, used)
        ids = jnp.pad(ids, ((0, 0), (0, 0), (0, LANES - used)), constant_values=-1)
        return jnp.broadcast_to(ids, (n, rhs, LANES))

    row_ids = spread(code // clusters % clusters)
    col_ids = spread(code % clusters)
    smem = pl.BlockSpec(memory_space=pltpu.SMEM)
    vmem = pl.BlockSpec(memory_space=pltpu.VMEM)
    hbm = pl.BlockSpec(memory_space=pl.ANY)
    dma = pltpu.SemaphoreType.DMA
    return pl.pallas_call(
        functools.partial(kernel, n, most, float(width * n)),
        out_shape=(
            jax.ShapeDtypeStruct((rhs, width), F32),
            jax.ShapeDtypeStruct((5, rhs), F32),
        ),
        in_specs=[smem, smem, vmem, vmem, vmem, vmem, hbm, hbm, hbm, hbm],
        out_specs=(vmem, vmem),
        scratch_shapes=[
            pltpu.VMEM(self_blocks.shape, BF16),
            pltpu.VMEM(near_blocks.shape, BF16),
            pltpu.VMEM(far_left.shape, BF16),
            pltpu.VMEM(far_right.shape, BF16),
            pltpu.VMEM((n, 2 * LANES, panels), BF16),
            pltpu.VMEM((n, used, panels), BF16),
            pltpu.VMEM((n, rhs, LANES), jnp.int32),
            pltpu.VMEM((REDUCTIONS, rhs, LANES), F32),
            pltpu.VMEM((REDUCTIONS, n, rhs, LANES), F32),
            pltpu.VMEM((2, flat, panels), BF16),
            pltpu.VMEM((2, 2, flat, panels), BF16),
            pltpu.VMEM((2, 2, flat, panels), BF16),
            pltpu.VMEM((2, 2, flat, panels), BF16),
            pltpu.VMEM((2, n, 2 * rhs, LANES), BF16),
            pltpu.VMEM((2, n, 2 * rhs, LANES), BF16),
            pltpu.VMEM((3 * clusters, rhs, panels), F32),
            pltpu.VMEM((pairs, rhs, panels), F32),
            pltpu.VMEM((2, clusters, rhs, panels), F32),
            dma((3 + NEAR_CHUNKS,)),
            dma((REDUCTIONS,)),
            dma((REDUCTIONS,)),
            dma((1,)), dma((1,)), dma((1,)), dma((1,)),
            dma((2, 2)), dma((2, 2)), dma((2, 2)), dma((2, 2)),
            dma((2,)), dma((2,)),
        ],
        compiler_params=pltpu.CompilerParams(
            collective_id=0, has_side_effects=True, vmem_limit_bytes=60 * 1024 * 1024
        ),
    )(near_ids, perm, start, keys, row_ids, col_ids, self_blocks, near_blocks, far_left, far_right)


def solution(mesh):
    in_specs = (
        P(None, "dev"),
        P("dev", None, None),
        P(None, "dev"),
        P("dev", None, None),
        P(None, "dev"),
        P("dev", None, None),
        P("dev", None, None),
    )
    out_specs = (P(None, "dev"), P())
    return jax.shard_map(
        per_device, mesh=mesh, in_specs=in_specs, out_specs=out_specs, check_vma=False
    )
```

```python
import functools
import jax
import jax.numpy as jnp
from jax import lax
from jax.experimental import pallas as pl
from jax.experimental.pallas import tpu as pltpu
from jax.sharding import PartitionSpec as P

epsilon = 1e-06
LANES = 128
MESH = pl.DeviceIdType.MESH
F32 = jnp.float32
BF16 = jnp.bfloat16
NEAR_CHUNKS = 4
REDUCTIONS = 3
STATS = 16
STRIDE = 13
TINY = 1e-20


def dot_nn(a, b):
    return lax.dot_general(a, b, (((1,), (0,)), ((), ())), preferred_element_type=F32)


def dot_nt(a, b):
    return lax.dot_general(a, b, (((1,), (1,)), ((), ())), preferred_element_type=F32)


def row_sum(a):
    return jnp.sum(jnp.sum(a, axis=0), axis=1, keepdims=True)


def one_hot_sum(keys, terms, groups):
    count = terms.shape[0]
    hot = jnp.where(lax.broadcasted_iota(jnp.int32, (groups, count), 0) == keys, 1.0, 0.0).astype(BF16)
    high = terms.astype(BF16)
    low = (terms - high.astype(F32)).astype(BF16)
    return dot_nn(hot, high) + dot_nn(hot, low)


def kernel(
    n, most, total_count,
    near_ids, perm, start_ref, keys_ref, row_ids, col_ids, self_hbm, near_hbm, left_hbm, right_hbm,
    out_ref, hess_ref,
    selfs, nears, lefts, rights, factors, outgoing, id_recv, stat_send, stat_recv,
    halo_send, halo_recv, part_send, part_recv, message, message_recv,
    extended, terms, basis,
    load_sem, stat_ssem, stat_rsem, fact_ssem, fact_rsem, id_ssem, id_rsem,
    halo_ssem, halo_rsem, part_ssem, part_rsem, msg_ssem, msg_rsem,
):
    me = lax.axis_index("dev")
    after = lax.rem(me + 1, n)
    before = lax.rem(me + n - 1, n)
    clusters, panels, _ = self_hbm.shape
    pairs = near_hbm.shape[0]
    rank = left_hbm.shape[1]
    rhs = start_ref.shape[0]
    used = most * rank
    flat = clusters * rhs

    def peer_loop(body):
        def step(i, carry):
            body(lax.rem(me + i * STRIDE, n))
            return carry
        lax.fori_loop(1, n, step, 0)

    def remote(src, dst, ssem, rsem, peer):
        return pltpu.make_async_remote_copy(
            src_ref=src, dst_ref=dst, send_sem=ssem, recv_sem=rsem,
            device_id=(peer,), device_id_type=MESH,
        )

    def wait_bytes(ref, sem):
        pltpu.make_async_copy(ref, ref, sem).wait()

    right_copy = pltpu.make_async_copy(right_hbm, rights, load_sem.at[0])
    right_copy.start()
    left_copy = pltpu.make_async_copy(left_hbm, lefts, load_sem.at[1])
    left_copy.start()
    loads = [pltpu.make_async_copy(self_hbm, selfs, load_sem.at[2])]
    size = pairs // NEAR_CHUNKS
    for part in range(NEAR_CHUNKS):
        span = pl.ds(part * size, size)
        loads.append(pltpu.make_async_copy(near_hbm.at[span], nears.at[span], load_sem.at[3 + part]))
    for load in loads:
        load.start()

    barrier = pltpu.get_barrier_semaphore()
    peer_loop(lambda peer: pl.semaphore_signal(barrier, inc=1, device_id=(peer,), device_id_type=MESH))

    eye = lax.broadcasted_iota(jnp.int32, (rhs, LANES), 0) == lax.broadcasted_iota(
        jnp.int32, (rhs, LANES), 1
    )

    def to_row(column):
        return jnp.sum(jnp.where(eye, column, 0.0), axis=0, keepdims=True)

    def to_column(row):
        return jnp.sum(jnp.where(eye, row, 0.0), axis=1, keepdims=True)

    def send_stats(index, columns):
        rows = [to_row(column) for column in columns]
        rows.append(jnp.zeros((STATS - len(rows), LANES), F32))
        block = jnp.concatenate(rows, axis=0)
        stat_send[index] = block
        stat_recv[index, me] = block
        peer_loop(lambda peer: remote(
            stat_send.at[index], stat_recv.at[index, me], stat_ssem.at[index], stat_rsem.at[index], peer
        ).start())

    def get_stats(index, count):
        wait_bytes(stat_recv.at[index, pl.ds(0, n - 1)], stat_rsem.at[index])
        return [stat_recv[index, :, place, :] for place in range(count)]

    def mean(terms):
        return jnp.sum(terms, axis=0, keepdims=True) / total_count

    first = jnp.stack([start_ref[:, c * panels:(c + 1) * panels] for c in range(clusters)], axis=0)
    partial = row_sum(first * first)

    id_recv[me] = jnp.full((rhs, LANES), -1, jnp.int32)
    if used < LANES:
        def clear(t, carry):
            factors[t] = jnp.zeros((2 * LANES, panels), BF16)
            return carry
        lax.fori_loop(0, n, clear, 0)
    else:
        factors[me] = jnp.zeros((2 * LANES, panels), BF16)
    for it in range(2):
        message_recv[it, me] = jnp.zeros((2 * rhs, LANES), BF16)

    pl.semaphore_wait(barrier, n - 1)
    send_stats(0, [partial])

    right_copy.wait()
    left_copy.wait()

    def send_factors(peer):
        for m in range(most):
            pair = perm[peer * most + m]
            outgoing[peer, pl.ds(m * rank, rank)] = rights[pair]
        remote(col_ids.at[peer], id_recv.at[me], id_ssem.at[0], id_rsem.at[0], peer).start()
        remote(
            outgoing.at[peer], factors.at[me, pl.ds(0, used)], fact_ssem.at[0], fact_rsem.at[0], peer
        ).start()
        for m in range(most):
            pair = perm[peer * most + m]
            factors[peer, pl.ds(LANES + m * rank, rank)] = lefts[pair]

    peer_loop(send_factors)

    (square,) = get_stats(0, 1)
    scale = to_column(jnp.sqrt(mean(square) + epsilon))
    basis[0] = first / scale[None]

    for load in loads:
        load.wait()

    heights = []
    for it in range(2):
        vector = basis[it].reshape(flat, panels).astype(BF16)
        halo_send[it] = vector
        halos = [
            remote(halo_send.at[it], halo_recv.at[it, 0], halo_ssem.at[it, 0], halo_rsem.at[it, 0], after),
            remote(halo_send.at[it], halo_recv.at[it, 1], halo_ssem.at[it, 1], halo_rsem.at[it, 1], before),
        ]
        for halo in halos:
            halo.start()
        extended[pl.ds(clusters, clusters)] = vector.astype(F32).reshape(clusters, rhs, panels)

        def exchange_far():
            if it == 0:
                wait_bytes(factors.at[pl.ds(0, n - 1), pl.ds(0, used)], fact_rsem.at[0])
                wait_bytes(id_recv.at[pl.ds(0, n - 1)], id_rsem.at[0])

            def products(t4, carry):
                for u in range(4):
                    t = t4 * 4 + u
                    e = dot_nt(vector, factors[t])
                    coeff = jnp.zeros((rhs, LANES), F32)
                    lean = jnp.zeros((rhs, LANES), F32)
                    for c in range(clusters):
                        rows = slice(c * rhs, (c + 1) * rhs)
                        coeff = jnp.where(id_recv[t] == c, e[rows, :LANES], coeff)
                        lean = jnp.where(row_ids[t] == c, e[rows, LANES:], lean)
                    message[it, t] = jnp.concatenate([coeff, lean], axis=0).astype(BF16)
                return carry

            lax.fori_loop(0, n // 4, products, 0)
            peer_loop(lambda peer: remote(
                message.at[it, peer], message_recv.at[it, me], msg_ssem.at[it], msg_rsem.at[it], peer
            ).start())

        if it == 1:
            exchange_far()

        def to_cols(p8, carry):
            for u in range(8):
                p = p8 * 8 + u
                x = extended[near_ids[0, p] + clusters].astype(BF16)
                terms[p] = dot_nn(x, nears[p])
            return carry

        lax.fori_loop(0, pairs // 8, to_cols, 0)
        sums = one_hot_sum(keys_ref[1:2, :], terms[...].reshape(pairs * rhs, panels), 3 * flat)
        part_send[it, 0] = sums[:flat].astype(BF16)
        part_send[it, 1] = sums[2 * flat:].astype(BF16)
        shares = [
            remote(part_send.at[it, 0], part_recv.at[it, 0], part_ssem.at[it, 0], part_rsem.at[it, 0], before),
            remote(part_send.at[it, 1], part_recv.at[it, 1], part_ssem.at[it, 1], part_rsem.at[it, 1], after),
        ]
        for share in shares:
            share.start()
        image = sums[flat:2 * flat]
        image = image + jnp.concatenate(
            [dot_nt(vector[c * rhs:(c + 1) * rhs], selfs[c]) for c in range(clusters)], axis=0
        )
        for halo in halos:
            halo.wait_recv()
        extended[pl.ds(0, clusters)] = halo_recv[it, 0].astype(F32).reshape(clusters, rhs, panels)
        extended[pl.ds(2 * clusters, clusters)] = halo_recv[it, 1].astype(F32).reshape(
            clusters, rhs, panels
        )

        def to_rows(p8, carry):
            for u in range(8):
                p = p8 * 8 + u
                x = extended[near_ids[1, p]].astype(BF16)
                terms[p] = dot_nt(x, nears[p])
            return carry

        lax.fori_loop(0, pairs // 8, to_rows, 0)
        image = image + one_hot_sum(keys_ref[0:1, :], terms[...].reshape(pairs * rhs, panels), flat)
        if it == 0:
            exchange_far()
        for share in shares:
            share.wait_recv()
        has_before = jnp.where(me > 0, 1.0, 0.0)
        has_after = jnp.where(me < n - 1, 1.0, 0.0)
        image = image + part_recv[it, 0].astype(F32) * has_after + part_recv[it, 1].astype(F32) * has_before
        wait_bytes(message_recv.at[it, pl.ds(0, n - 1)], msg_rsem.at[it])

        def far_terms(t4, total):
            for u in range(4):
                t = t4 * 4 + u
                arrived = message_recv[it, t].astype(F32)
                coeff, lean = arrived[:rhs], arrived[rhs:]
                spread = jnp.concatenate(
                    [
                        jnp.concatenate(
                            [
                                jnp.where(id_recv[t] == c, lean, 0.0),
                                jnp.where(row_ids[t] == c, coeff, 0.0),
                            ],
                            axis=1,
                        )
                        for c in range(clusters)
                    ],
                    axis=0,
                ).astype(BF16)
                total = total + dot_nn(spread, factors[t])
            return total

        image = lax.fori_loop(0, n // 4, far_terms, image).reshape(clusters, rhs, panels)

        count = it + 1
        vectors = [basis[b] for b in range(count)]
        inner = [row_sum(v * image) for v in vectors]
        gram = [row_sum(vectors[b] * vectors[d]) for b in range(count) for d in range(b, count)]
        diagonal = [gram[0]] if it == 0 else [gram[0], gram[2]]
        near_rest = image
        guesses = []
        for b in range(count):
            product = inner[0] if b == 0 else row_sum(vectors[b] * near_rest)
            wide = diagonal[b] > TINY
            guess = jnp.where(wide, product / jnp.where(wide, diagonal[b], 1.0), 0.0)
            near_rest = near_rest - guess[None] * vectors[b]
            guesses.append(guess)
        left_over = [row_sum(v * near_rest) for v in vectors]
        columns = inner + guesses + left_over + gram + [row_sum(near_rest * near_rest)]
        send_stats(1 + it, columns)
        got = get_stats(1 + it, len(columns))
        rows = [mean(got[b]) for b in range(count)]
        change = [rows[b] - got[count + b] for b in range(count)]
        square = got[-1]
        for b in range(count):
            square = square - 2.0 * change[b] * got[2 * count + b]
        place = 3 * count
        for b in range(count):
            for d in range(b, count):
                square = square + (1.0 if b == d else 2.0) * change[b] * change[d] * got[place]
                place += 1
        norm = jnp.sqrt(jnp.maximum(mean(square), 0.0) + epsilon)
        rest = image
        for b in range(count):
            rest = rest - to_column(rows[b])[None] * vectors[b]
        heights.extend(rows)
        heights.append(norm)
        following = rest / to_column(norm)[None]
        if it == 0:
            basis[1] = following
        else:
            for c in range(clusters):
                out_ref[:, c * panels:(c + 1) * panels] = following[c]

    for place, height in enumerate(heights):
        hess_ref[place:place + 1, :] = height[:, :rhs]

    for index in range(REDUCTIONS):
        wait_bytes(stat_recv.at[index, pl.ds(0, n - 1)], stat_ssem.at[index])
    wait_bytes(factors.at[pl.ds(0, n - 1), pl.ds(0, used)], fact_ssem.at[0])
    wait_bytes(id_recv.at[pl.ds(0, n - 1)], id_ssem.at[0])
    for it in range(2):
        for side in range(2):
            wait_bytes(halo_send.at[it], halo_ssem.at[it, side])
            wait_bytes(part_send.at[it, side], part_ssem.at[it, side])
        wait_bytes(message_recv.at[it, pl.ds(0, n - 1)], msg_ssem.at[it])


def per_device(start, self_blocks, near_pairs, near_blocks, far_pairs, far_left, far_right):
    n = lax.axis_size("dev")
    me = lax.axis_index("dev")
    rhs, width = start.shape
    clusters, panels, _ = self_blocks.shape
    pairs = near_pairs.shape[1]
    far_count = far_pairs.shape[1]
    rank = far_left.shape[1]
    most = max(2, 2 * far_count // n)
    used = most * rank
    flat = clusters * rhs
    near_rows = near_pairs[0] - me * clusters
    near_cols = near_pairs[1] - (me - 1) * clusters
    near_ids = jnp.stack([near_rows, near_cols])
    keys = (near_ids[:, :, None] * rhs + jnp.arange(rhs, dtype=jnp.int32)).reshape(2, pairs * rhs)
    target = far_pairs[1] // clusters
    order = jnp.arange(far_count, dtype=jnp.int32)
    earlier = (target[:, None] == target[None, :]) & (order[None, :] < order[:, None])
    slot = target * most + jnp.sum(earlier.astype(jnp.int32), axis=1)
    hit = slot[None, :] == jnp.arange(n * most, dtype=jnp.int32)[:, None]
    code = order * (clusters * clusters) + (far_pairs[0] - me * clusters) * clusters + far_pairs[1] % clusters
    code = jnp.sum(jnp.where(hit, code[None, :] + 1, 0), axis=1) - 1
    filled = code >= 0
    perm = jnp.where(filled, code // (clusters * clusters), 0)

    def spread(ids):
        ids = jnp.where(filled, ids, -1).reshape(n, most, 1)
        ids = jnp.broadcast_to(ids, (n, most, rank)).reshape(n, 1, used)
        ids = jnp.pad(ids, ((0, 0), (0, 0), (0, LANES - used)), constant_values=-1)
        return jnp.broadcast_to(ids, (n, rhs, LANES))

    row_ids = spread(code // clusters % clusters)
    col_ids = spread(code % clusters)
    smem = pl.BlockSpec(memory_space=pltpu.SMEM)
    vmem = pl.BlockSpec(memory_space=pltpu.VMEM)
    hbm = pl.BlockSpec(memory_space=pl.ANY)
    dma = pltpu.SemaphoreType.DMA
    return pl.pallas_call(
        functools.partial(kernel, n, most, float(width * n)),
        out_shape=(
            jax.ShapeDtypeStruct((rhs, width), F32),
            jax.ShapeDtypeStruct((5, rhs), F32),
        ),
        in_specs=[smem, smem, vmem, vmem, vmem, vmem, hbm, hbm, hbm, hbm],
        out_specs=(vmem, vmem),
        scratch_shapes=[
            pltpu.VMEM(self_blocks.shape, BF16),
            pltpu.VMEM(near_blocks.shape, BF16),
            pltpu.VMEM(far_left.shape, BF16),
            pltpu.VMEM(far_right.shape, BF16),
            pltpu.VMEM((n, 2 * LANES, panels), BF16),
            pltpu.VMEM((n, used, panels), BF16),
            pltpu.VMEM((n, rhs, LANES), jnp.int32),
            pltpu.VMEM((REDUCTIONS, STATS, LANES), F32),
            pltpu.VMEM((REDUCTIONS, n, STATS, LANES), F32),
            pltpu.VMEM((2, flat, panels), BF16),
            pltpu.VMEM((2, 2, flat, panels), BF16),
            pltpu.VMEM((2, 2, flat, panels), BF16),
            pltpu.VMEM((2, 2, flat, panels), BF16),
            pltpu.VMEM((2, n, 2 * rhs, LANES), BF16),
            pltpu.VMEM((2, n, 2 * rhs, LANES), BF16),
            pltpu.VMEM((3 * clusters, rhs, panels), F32),
            pltpu.VMEM((pairs, rhs, panels), F32),
            pltpu.VMEM((2, clusters, rhs, panels), F32),
            dma((3 + NEAR_CHUNKS,)),
            dma((REDUCTIONS,)),
            dma((REDUCTIONS,)),
            dma((1,)), dma((1,)), dma((1,)), dma((1,)),
            dma((2, 2)), dma((2, 2)), dma((2, 2)), dma((2, 2)),
            dma((2,)), dma((2,)),
        ],
        compiler_params=pltpu.CompilerParams(
            collective_id=0, has_side_effects=True, vmem_limit_bytes=60 * 1024 * 1024
        ),
    )(near_ids, perm, start, keys, row_ids, col_ids, self_blocks, near_blocks, far_left, far_right)


def solution(mesh):
    in_specs = (
        P(None, "dev"),
        P("dev", None, None),
        P(None, "dev"),
        P("dev", None, None),
        P(None, "dev"),
        P("dev", None, None),
        P("dev", None, None),
    )
    out_specs = (P(None, "dev"), P())
    return jax.shard_map(
        per_device, mesh=mesh, in_specs=in_specs, out_specs=out_specs, check_vma=False
    )
```

```python
import functools
import jax
import jax.numpy as jnp
from jax import lax
from jax.experimental import pallas as pl
from jax.experimental.pallas import tpu as pltpu
from jax.sharding import PartitionSpec as P

epsilon = 1e-06
LANES = 128
MESH = pl.DeviceIdType.MESH
F32 = jnp.float32
BF16 = jnp.bfloat16
NEAR_CHUNKS = 4
REDUCTIONS = 3
STATS = 16
STRIDE = 13
TINY = 1e-20


def dot_nn(a, b):
    return lax.dot_general(a, b, (((1,), (0,)), ((), ())), preferred_element_type=F32)


def dot_nt(a, b):
    return lax.dot_general(a, b, (((1,), (1,)), ((), ())), preferred_element_type=F32)


def row_sum(a):
    return jnp.sum(jnp.sum(a, axis=0), axis=1, keepdims=True)


def one_hot_sum(keys, terms, groups):
    count = terms.shape[0]
    hot = jnp.where(lax.broadcasted_iota(jnp.int32, (groups, count), 0) == keys, 1.0, 0.0).astype(BF16)
    high = terms.astype(BF16)
    low = (terms - high.astype(F32)).astype(BF16)
    return dot_nn(hot, high) + dot_nn(hot, low)


def kernel(
    n, most, total_count,
    near_ids, perm, start_ref, keys_ref, row_ids, col_ids, self_hbm, near_hbm, left_hbm, right_hbm,
    out_ref, hess_ref,
    selfs, nears, lefts, rights, factors, outgoing, id_recv, stat_send, stat_recv,
    raw_recv, halo_send, halo_recv, part_send, part_recv, message, message_recv,
    extended, terms, basis,
    load_sem, raw_ssem, raw_rsem, stat_ssem, stat_rsem, fact_ssem, fact_rsem, id_ssem, id_rsem,
    halo_ssem, halo_rsem, part_ssem, part_rsem, msg_ssem, msg_rsem,
):
    me = lax.axis_index("dev")
    after = lax.rem(me + 1, n)
    before = lax.rem(me + n - 1, n)
    clusters, panels, _ = self_hbm.shape
    pairs = near_hbm.shape[0]
    rank = left_hbm.shape[1]
    rhs = start_ref.shape[0]
    used = most * rank
    flat = clusters * rhs

    def peer_loop(body, unroll=True):
        def step(i, carry):
            body(lax.rem(me + i * STRIDE, n))
            return carry
        lax.fori_loop(1, n, step, 0, unroll=unroll and n <= 32)

    def remote(src, dst, ssem, rsem, peer):
        return pltpu.make_async_remote_copy(
            src_ref=src, dst_ref=dst, send_sem=ssem, recv_sem=rsem,
            device_id=(peer,), device_id_type=MESH,
        )

    def wait_bytes(ref, sem):
        pltpu.make_async_copy(ref, ref, sem).wait()

    right_copy = pltpu.make_async_copy(right_hbm, rights, load_sem.at[0])
    right_copy.start()
    left_copy = pltpu.make_async_copy(left_hbm, lefts, load_sem.at[1])
    left_copy.start()
    loads = [pltpu.make_async_copy(self_hbm, selfs, load_sem.at[2])]
    size = pairs // NEAR_CHUNKS
    for part in range(NEAR_CHUNKS):
        span = pl.ds(part * size, size)
        loads.append(pltpu.make_async_copy(near_hbm.at[span], nears.at[span], load_sem.at[3 + part]))
    for load in loads:
        load.start()

    barrier = pltpu.get_barrier_semaphore()
    peer_loop(lambda peer: pl.semaphore_signal(barrier, inc=1, device_id=(peer,), device_id_type=MESH))

    eye = lax.broadcasted_iota(jnp.int32, (rhs, LANES), 0) == lax.broadcasted_iota(
        jnp.int32, (rhs, LANES), 1
    )

    def to_row(column):
        return jnp.sum(jnp.where(eye, column, 0.0), axis=0, keepdims=True)

    def to_column(row):
        return jnp.sum(jnp.where(eye, row, 0.0), axis=1, keepdims=True)

    def send_stats(index, columns):
        rows = [to_row(column) for column in columns]
        rows.append(jnp.zeros((STATS - len(rows), LANES), F32))
        block = jnp.concatenate(rows, axis=0)
        stat_send[index] = block
        stat_recv[index, me] = block
        peer_loop(lambda peer: remote(
            stat_send.at[index], stat_recv.at[index, me], stat_ssem.at[index], stat_rsem.at[index], peer
        ).start())

    def get_stats(index, count):
        wait_bytes(stat_recv.at[index, pl.ds(0, n - 1)], stat_rsem.at[index])
        return [stat_recv[index, :, place, :] for place in range(count)]

    def mean(terms):
        return jnp.sum(terms, axis=0, keepdims=True) / total_count

    first = jnp.stack([start_ref[:, c * panels:(c + 1) * panels] for c in range(clusters)], axis=0)
    partial = row_sum(first * first)

    id_recv[me] = jnp.full((rhs, LANES), -1, jnp.int32)
    if used < LANES:
        def clear(t, carry):
            factors[t] = jnp.zeros((2 * LANES, panels), BF16)
            return carry
        lax.fori_loop(0, n, clear, 0)
    else:
        factors[me] = jnp.zeros((2 * LANES, panels), BF16)
    for it in range(2):
        message_recv[it, me] = jnp.zeros((2 * rhs, LANES), BF16)

    pl.semaphore_wait(barrier, n - 1)
    send_stats(0, [partial])
    raws = [
        remote(start_ref, raw_recv.at[0], raw_ssem.at[0], raw_rsem.at[0], after),
        remote(start_ref, raw_recv.at[1], raw_ssem.at[1], raw_rsem.at[1], before),
    ]
    for raw in raws:
        raw.start()

    right_copy.wait()
    left_copy.wait()

    def send_factors(peer):
        for m in range(most):
            pair = perm[peer * most + m]
            outgoing[peer, pl.ds(m * rank, rank)] = rights[pair]
        remote(col_ids.at[peer], id_recv.at[me], id_ssem.at[0], id_rsem.at[0], peer).start()
        remote(
            outgoing.at[peer], factors.at[me, pl.ds(0, used)], fact_ssem.at[0], fact_rsem.at[0], peer
        ).start()

    peer_loop(send_factors, False)

    def place_left(peer):
        for m in range(most):
            pair = perm[peer * most + m]
            factors[peer, pl.ds(LANES + m * rank, rank)] = lefts[pair]

    peer_loop(place_left, False)

    (square,) = get_stats(0, 1)
    scale = to_column(jnp.sqrt(mean(square) + epsilon))
    basis[0] = first / scale[None]

    for load in loads:
        load.wait()

    heights = []
    for it in range(2):
        vector = basis[it].reshape(flat, panels).astype(BF16)
        if it == 0:
            halos = raws
        else:
            halo_send[...] = vector
            halos = [
                remote(halo_send, halo_recv.at[0], halo_ssem.at[0], halo_rsem.at[0], after),
                remote(halo_send, halo_recv.at[1], halo_ssem.at[1], halo_rsem.at[1], before),
            ]
            for halo in halos:
                halo.start()
        extended[pl.ds(clusters, clusters)] = vector.astype(F32).reshape(clusters, rhs, panels)

        def exchange_far():
            if it == 0:
                wait_bytes(factors.at[pl.ds(0, n - 1), pl.ds(0, used)], fact_rsem.at[0])
                wait_bytes(id_recv.at[pl.ds(0, n - 1)], id_rsem.at[0])

            def products(t8, carry):
                for u in range(8):
                    t = t8 * 8 + u
                    e = dot_nt(vector, factors[t])
                    coeff = jnp.zeros((rhs, LANES), F32)
                    lean = jnp.zeros((rhs, LANES), F32)
                    for c in range(clusters):
                        rows = slice(c * rhs, (c + 1) * rhs)
                        coeff = jnp.where(id_recv[t] == c, e[rows, :LANES], coeff)
                        lean = jnp.where(row_ids[t] == c, e[rows, LANES:], lean)
                    message[it, t] = jnp.concatenate([coeff, lean], axis=0).astype(BF16)
                return carry

            lax.fori_loop(0, n // 8, products, 0)
            peer_loop(lambda peer: remote(
                message.at[it, peer], message_recv.at[it, me], msg_ssem.at[it], msg_rsem.at[it], peer
            ).start())

        if it == 1:
            exchange_far()

        def to_cols(p8, carry):
            for u in range(16):
                p = p8 * 16 + u
                x = extended[near_ids[0, p] + clusters].astype(BF16)
                terms[p] = dot_nn(x, nears[p])
            return carry

        lax.fori_loop(0, pairs // 16, to_cols, 0)
        sums = one_hot_sum(keys_ref[1:2, :], terms[...].reshape(pairs * rhs, panels), 3 * flat)
        part_send[it, 0] = sums[:flat].astype(BF16)
        part_send[it, 1] = sums[2 * flat:].astype(BF16)
        shares = [
            remote(part_send.at[it, 0], part_recv.at[it, 0], part_ssem.at[it, 0], part_rsem.at[it, 0], before),
            remote(part_send.at[it, 1], part_recv.at[it, 1], part_ssem.at[it, 1], part_rsem.at[it, 1], after),
        ]
        for share in shares:
            share.start()
        image = sums[flat:2 * flat]
        image = image + jnp.concatenate(
            [dot_nt(vector[c * rhs:(c + 1) * rhs], selfs[c]) for c in range(clusters)], axis=0
        )
        for halo in halos:
            halo.wait_recv()
        for side in range(2):
            if it == 0:
                for c in range(clusters):
                    raw = raw_recv[side, :, c * panels:(c + 1) * panels]
                    extended[2 * clusters * side + c] = raw / scale
            else:
                extended[pl.ds(2 * clusters * side, clusters)] = halo_recv[side].astype(F32).reshape(
                    clusters, rhs, panels
                )

        def to_rows(p8, carry):
            for u in range(16):
                p = p8 * 16 + u
                x = extended[near_ids[1, p]].astype(BF16)
                terms[p] = dot_nt(x, nears[p])
            return carry

        lax.fori_loop(0, pairs // 16, to_rows, 0)
        image = image + one_hot_sum(keys_ref[0:1, :], terms[...].reshape(pairs * rhs, panels), flat)
        if it == 0:
            exchange_far()
        for share in shares:
            share.wait_recv()
        has_before = jnp.where(me > 0, 1.0, 0.0)
        has_after = jnp.where(me < n - 1, 1.0, 0.0)
        image = image + part_recv[it, 0].astype(F32) * has_after + part_recv[it, 1].astype(F32) * has_before
        wait_bytes(message_recv.at[it, pl.ds(0, n - 1)], msg_rsem.at[it])

        def far_terms(t8, total):
            for u in range(8):
                t = t8 * 8 + u
                arrived = message_recv[it, t].astype(F32)
                coeff, lean = arrived[:rhs], arrived[rhs:]
                spread = jnp.concatenate(
                    [
                        jnp.concatenate(
                            [
                                jnp.where(id_recv[t] == c, lean, 0.0),
                                jnp.where(row_ids[t] == c, coeff, 0.0),
                            ],
                            axis=1,
                        )
                        for c in range(clusters)
                    ],
                    axis=0,
                ).astype(BF16)
                total = total + dot_nn(spread, factors[t])
            return total

        image = lax.fori_loop(0, n // 8, far_terms, image).reshape(clusters, rhs, panels)

        count = it + 1
        vectors = [basis[b] for b in range(count)]
        inner = [row_sum(v * image) for v in vectors]
        gram = [row_sum(vectors[b] * vectors[d]) for b in range(count) for d in range(b, count)]
        diagonal = [gram[0]] if it == 0 else [gram[0], gram[2]]
        near_rest = image
        guesses = []
        for b in range(count):
            product = inner[0] if b == 0 else row_sum(vectors[b] * near_rest)
            wide = diagonal[b] > TINY
            guess = jnp.where(wide, product / jnp.where(wide, diagonal[b], 1.0), 0.0)
            near_rest = near_rest - guess[None] * vectors[b]
            guesses.append(guess)
        left_over = [row_sum(v * near_rest) for v in vectors]
        columns = inner + guesses + left_over + gram + [row_sum(near_rest * near_rest)]
        send_stats(1 + it, columns)
        got = get_stats(1 + it, len(columns))
        rows = [mean(got[b]) for b in range(count)]
        change = [rows[b] - got[count + b] for b in range(count)]
        square = got[-1]
        for b in range(count):
            square = square - 2.0 * change[b] * got[2 * count + b]
        place = 3 * count
        for b in range(count):
            for d in range(b, count):
                square = square + (1.0 if b == d else 2.0) * change[b] * change[d] * got[place]
                place += 1
        norm = jnp.sqrt(jnp.maximum(mean(square), 0.0) + epsilon)
        rest = image
        for b in range(count):
            rest = rest - to_column(rows[b])[None] * vectors[b]
        heights.extend(rows)
        heights.append(norm)
        following = rest / to_column(norm)[None]
        if it == 0:
            basis[1] = following
        else:
            for c in range(clusters):
                out_ref[:, c * panels:(c + 1) * panels] = following[c]

    for place, height in enumerate(heights):
        hess_ref[place:place + 1, :] = height[:, :rhs]

    for index in range(REDUCTIONS):
        wait_bytes(stat_recv.at[index, pl.ds(0, n - 1)], stat_ssem.at[index])
    wait_bytes(factors.at[pl.ds(0, n - 1), pl.ds(0, used)], fact_ssem.at[0])
    wait_bytes(id_recv.at[pl.ds(0, n - 1)], id_ssem.at[0])
    for side in range(2):
        wait_bytes(start_ref, raw_ssem.at[side])
        wait_bytes(halo_send, halo_ssem.at[side])
    for it in range(2):
        for side in range(2):
            wait_bytes(part_send.at[it, side], part_ssem.at[it, side])
        wait_bytes(message_recv.at[it, pl.ds(0, n - 1)], msg_ssem.at[it])


def per_device(start, self_blocks, near_pairs, near_blocks, far_pairs, far_left, far_right):
    n = lax.axis_size("dev")
    me = lax.axis_index("dev")
    rhs, width = start.shape
    clusters, panels, _ = self_blocks.shape
    pairs = near_pairs.shape[1]
    far_count = far_pairs.shape[1]
    rank = far_left.shape[1]
    most = max(2, 2 * far_count // n)
    used = most * rank
    flat = clusters * rhs
    near_rows = near_pairs[0] - me * clusters
    near_cols = near_pairs[1] - (me - 1) * clusters
    near_ids = jnp.stack([near_rows, near_cols])
    keys = (near_ids[:, :, None] * rhs + jnp.arange(rhs, dtype=jnp.int32)).reshape(2, pairs * rhs)
    target = far_pairs[1] // clusters
    order = jnp.arange(far_count, dtype=jnp.int32)
    earlier = (target[:, None] == target[None, :]) & (order[None, :] < order[:, None])
    slot = target * most + jnp.sum(earlier.astype(jnp.int32), axis=1)
    hit = slot[None, :] == jnp.arange(n * most, dtype=jnp.int32)[:, None]
    code = order * (clusters * clusters) + (far_pairs[0] - me * clusters) * clusters + far_pairs[1] % clusters
    code = jnp.sum(jnp.where(hit, code[None, :] + 1, 0), axis=1) - 1
    filled = code >= 0
    perm = jnp.where(filled, code // (clusters * clusters), 0)

    def spread(ids):
        ids = jnp.where(filled, ids, -1).reshape(n, most, 1)
        ids = jnp.broadcast_to(ids, (n, most, rank)).reshape(n, 1, used)
        ids = jnp.pad(ids, ((0, 0), (0, 0), (0, LANES - used)), constant_values=-1)
        return jnp.broadcast_to(ids, (n, rhs, LANES))

    row_ids = spread(code // clusters % clusters)
    col_ids = spread(code % clusters)
    smem = pl.BlockSpec(memory_space=pltpu.SMEM)
    vmem = pl.BlockSpec(memory_space=pltpu.VMEM)
    hbm = pl.BlockSpec(memory_space=pl.ANY)
    dma = pltpu.SemaphoreType.DMA
    return pl.pallas_call(
        functools.partial(kernel, n, most, float(width * n)),
        out_shape=(
            jax.ShapeDtypeStruct((rhs, width), F32),
            jax.ShapeDtypeStruct((5, rhs), F32),
        ),
        in_specs=[smem, smem, vmem, vmem, vmem, vmem, hbm, hbm, hbm, hbm],
        out_specs=(vmem, vmem),
        scratch_shapes=[
            pltpu.VMEM(self_blocks.shape, BF16),
            pltpu.VMEM(near_blocks.shape, BF16),
            pltpu.VMEM(far_left.shape, BF16),
            pltpu.VMEM(far_right.shape, BF16),
            pltpu.VMEM((n, 2 * LANES, panels), BF16),
            pltpu.VMEM((n, used, panels), BF16),
            pltpu.VMEM((n, rhs, LANES), jnp.int32),
            pltpu.VMEM((REDUCTIONS, STATS, LANES), F32),
            pltpu.VMEM((REDUCTIONS, n, STATS, LANES), F32),
            pltpu.VMEM((2, rhs, width), F32),
            pltpu.VMEM((flat, panels), BF16),
            pltpu.VMEM((2, flat, panels), BF16),
            pltpu.VMEM((2, 2, flat, panels), BF16),
            pltpu.VMEM((2, 2, flat, panels), BF16),
            pltpu.VMEM((2, n, 2 * rhs, LANES), BF16),
            pltpu.VMEM((2, n, 2 * rhs, LANES), BF16),
            pltpu.VMEM((3 * clusters, rhs, panels), F32),
            pltpu.VMEM((pairs, rhs, panels), F32),
            pltpu.VMEM((2, clusters, rhs, panels), F32),
            dma((3 + NEAR_CHUNKS,)),
            dma((2,)), dma((2,)),
            dma((REDUCTIONS,)),
            dma((REDUCTIONS,)),
            dma((1,)), dma((1,)), dma((1,)), dma((1,)),
            dma((2,)), dma((2,)), dma((2, 2)), dma((2, 2)),
            dma((2,)), dma((2,)),
        ],
        compiler_params=pltpu.CompilerParams(
            collective_id=0, has_side_effects=True, vmem_limit_bytes=60 * 1024 * 1024
        ),
    )(near_ids, perm, start, keys, row_ids, col_ids, self_blocks, near_blocks, far_left, far_right)


def solution(mesh):
    in_specs = (
        P(None, "dev"),
        P("dev", None, None),
        P(None, "dev"),
        P("dev", None, None),
        P(None, "dev"),
        P("dev", None, None),
        P("dev", None, None),
    )
    out_specs = (P(None, "dev"), P())
    return jax.shard_map(
        per_device, mesh=mesh, in_specs=in_specs, out_specs=out_specs, check_vma=False
    )
```

```python
import functools
import jax
import jax.numpy as jnp
from jax import lax
from jax.experimental import pallas as pl
from jax.experimental.pallas import tpu as pltpu
from jax.sharding import PartitionSpec as P

epsilon = 1e-06
LANES = 128
MESH = pl.DeviceIdType.MESH
F32 = jnp.float32
BF16 = jnp.bfloat16
NEAR_CHUNKS = 4
REDUCTIONS = 3
STATS = 16
STRIDE = 13
TINY = 1e-20


def dot_nn(a, b):
    return lax.dot_general(a, b, (((1,), (0,)), ((), ())), preferred_element_type=F32)


def dot_nt(a, b):
    return lax.dot_general(a, b, (((1,), (1,)), ((), ())), preferred_element_type=F32)


def row_sum(a):
    return jnp.sum(jnp.sum(a, axis=0), axis=1, keepdims=True)


def one_hot_sum(keys, terms, groups):
    count = terms.shape[0]
    hot = jnp.where(lax.broadcasted_iota(jnp.int32, (groups, count), 0) == keys, 1.0, 0.0).astype(BF16)
    high = terms.astype(BF16)
    low = (terms - high.astype(F32)).astype(BF16)
    return dot_nn(hot, high) + dot_nn(hot, low)


def kernel(
    n, most, total_count,
    near_ids, perm, start_ref, keys_ref, row_ids, col_ids, self_hbm, near_hbm, left_hbm, right_hbm,
    out_ref, hess_ref,
    selfs, nears, lefts, rights, factors, outgoing, id_recv, stat_send, stat_recv,
    raw_recv, halo_send, halo_recv, part_send, part_recv, message, message_recv,
    extended, terms, basis,
    load_sem, raw_ssem, raw_rsem, stat_ssem, stat_rsem, fact_ssem, fact_rsem, id_ssem, id_rsem,
    halo_ssem, halo_rsem, part_ssem, part_rsem, msg_ssem, msg_rsem,
):
    me = lax.axis_index("dev")
    after = lax.rem(me + 1, n)
    before = lax.rem(me + n - 1, n)
    clusters, panels, _ = self_hbm.shape
    pairs = near_hbm.shape[0]
    rank = left_hbm.shape[1]
    rhs = start_ref.shape[0]
    used = most * rank
    flat = clusters * rhs

    def peer_loop(body, unroll=True):
        def step(i, carry):
            body(lax.rem(me + i * STRIDE, n))
            return carry
        lax.fori_loop(1, n, step, 0, unroll=unroll and n <= 32)

    def remote(src, dst, ssem, rsem, peer):
        return pltpu.make_async_remote_copy(
            src_ref=src, dst_ref=dst, send_sem=ssem, recv_sem=rsem,
            device_id=(peer,), device_id_type=MESH,
        )

    def wait_bytes(ref, sem):
        pltpu.make_async_copy(ref, ref, sem).wait()

    right_copy = pltpu.make_async_copy(right_hbm, rights, load_sem.at[0])
    right_copy.start()
    left_copy = pltpu.make_async_copy(left_hbm, lefts, load_sem.at[1])
    left_copy.start()
    loads = [pltpu.make_async_copy(self_hbm, selfs, load_sem.at[2])]
    size = pairs // NEAR_CHUNKS
    for part in range(NEAR_CHUNKS):
        span = pl.ds(part * size, size)
        loads.append(pltpu.make_async_copy(near_hbm.at[span], nears.at[span], load_sem.at[3 + part]))
    for load in loads:
        load.start()

    barrier = pltpu.get_barrier_semaphore()
    peer_loop(lambda peer: pl.semaphore_signal(barrier, inc=1, device_id=(peer,), device_id_type=MESH))

    eye = lax.broadcasted_iota(jnp.int32, (rhs, LANES), 0) == lax.broadcasted_iota(
        jnp.int32, (rhs, LANES), 1
    )

    def to_row(column):
        return jnp.sum(jnp.where(eye, column, 0.0), axis=0, keepdims=True)

    def to_column(row):
        return jnp.sum(jnp.where(eye, row, 0.0), axis=1, keepdims=True)

    def send_stats(index, columns):
        rows = [to_row(column) for column in columns]
        rows.append(jnp.zeros((STATS - len(rows), LANES), F32))
        block = jnp.concatenate(rows, axis=0)
        stat_send[index] = block
        stat_recv[index, me] = block
        peer_loop(lambda peer: remote(
            stat_send.at[index], stat_recv.at[index, me], stat_ssem.at[index], stat_rsem.at[index], peer
        ).start())

    def get_stats(index, count):
        wait_bytes(stat_recv.at[index, pl.ds(0, n - 1)], stat_rsem.at[index])
        return [stat_recv[index, :, place, :] for place in range(count)]

    def mean(terms):
        return jnp.sum(terms, axis=0, keepdims=True) / total_count

    first = jnp.stack([start_ref[:, c * panels:(c + 1) * panels] for c in range(clusters)], axis=0)
    partial = row_sum(first * first)

    id_recv[me] = jnp.full((rhs, LANES), -1, jnp.int32)
    if used < LANES:
        def clear(t, carry):
            factors[t] = jnp.zeros((2 * LANES, panels), BF16)
            return carry
        lax.fori_loop(0, n, clear, 0)
    else:
        factors[me] = jnp.zeros((2 * LANES, panels), BF16)
    for it in range(2):
        message_recv[it, me] = jnp.zeros((2 * rhs, LANES), BF16)

    pl.semaphore_wait(barrier, n - 1)
    send_stats(0, [partial])
    raws = [
        remote(start_ref, raw_recv.at[0], raw_ssem.at[0], raw_rsem.at[0], after),
        remote(start_ref, raw_recv.at[1], raw_ssem.at[1], raw_rsem.at[1], before),
    ]
    for raw in raws:
        raw.start()

    right_copy.wait()
    left_copy.wait()

    def send_factors(peer):
        for m in range(most):
            pair = perm[peer * most + m]
            outgoing[peer, pl.ds(m * rank, rank)] = rights[pair]
        remote(col_ids.at[peer], id_recv.at[me], id_ssem.at[0], id_rsem.at[0], peer).start()
        remote(
            outgoing.at[peer], factors.at[me, pl.ds(0, used)], fact_ssem.at[0], fact_rsem.at[0], peer
        ).start()

    peer_loop(send_factors, False)

    def place_left(peer):
        for m in range(most):
            pair = perm[peer * most + m]
            factors[peer, pl.ds(LANES + m * rank, rank)] = lefts[pair]

    peer_loop(place_left, False)

    (square,) = get_stats(0, 1)
    scale = to_column(jnp.sqrt(mean(square) + epsilon))
    basis[0] = first / scale[None]

    for load in loads:
        load.wait()

    heights = []
    for it in range(2):
        vector = basis[it].reshape(flat, panels).astype(BF16)
        if it == 0:
            halos = raws
        else:
            halo_send[...] = vector
            halos = [
                remote(halo_send, halo_recv.at[0], halo_ssem.at[0], halo_rsem.at[0], after),
                remote(halo_send, halo_recv.at[1], halo_ssem.at[1], halo_rsem.at[1], before),
            ]
            for halo in halos:
                halo.start()
        extended[pl.ds(clusters, clusters)] = vector.astype(F32).reshape(clusters, rhs, panels)

        def exchange_far():
            if it == 0:
                wait_bytes(factors.at[pl.ds(0, n - 1), pl.ds(0, used)], fact_rsem.at[0])
                wait_bytes(id_recv.at[pl.ds(0, n - 1)], id_rsem.at[0])

            def products(t8, carry):
                for u in range(16):
                    t = t8 * 16 + u
                    e = dot_nt(vector, factors[t])
                    coeff = jnp.zeros((rhs, LANES), F32)
                    lean = jnp.zeros((rhs, LANES), F32)
                    for c in range(clusters):
                        rows = slice(c * rhs, (c + 1) * rhs)
                        coeff = jnp.where(id_recv[t] == c, e[rows, :LANES], coeff)
                        lean = jnp.where(row_ids[t] == c, e[rows, LANES:], lean)
                    message[it, t] = jnp.concatenate([coeff, lean], axis=0).astype(BF16)
                return carry

            lax.fori_loop(0, n // 16, products, 0)
            peer_loop(lambda peer: remote(
                message.at[it, peer], message_recv.at[it, me], msg_ssem.at[it], msg_rsem.at[it], peer
            ).start())

        if it == 1:
            exchange_far()

        def to_cols(p8, carry):
            for u in range(32):
                p = p8 * 32 + u
                x = extended[near_ids[0, p] + clusters].astype(BF16)
                terms[p] = dot_nn(x, nears[p])
            return carry

        lax.fori_loop(0, pairs // 32, to_cols, 0)
        sums = one_hot_sum(keys_ref[1:2, :], terms[...].reshape(pairs * rhs, panels), 3 * flat)
        part_send[it, 0] = sums[:flat].astype(BF16)
        part_send[it, 1] = sums[2 * flat:].astype(BF16)
        shares = [
            remote(part_send.at[it, 0], part_recv.at[it, 0], part_ssem.at[it, 0], part_rsem.at[it, 0], before),
            remote(part_send.at[it, 1], part_recv.at[it, 1], part_ssem.at[it, 1], part_rsem.at[it, 1], after),
        ]
        for share in shares:
            share.start()
        image = sums[flat:2 * flat]
        image = image + jnp.concatenate(
            [dot_nt(vector[c * rhs:(c + 1) * rhs], selfs[c]) for c in range(clusters)], axis=0
        )
        for halo in halos:
            halo.wait_recv()
        for side in range(2):
            if it == 0:
                for c in range(clusters):
                    raw = raw_recv[side, :, c * panels:(c + 1) * panels]
                    extended[2 * clusters * side + c] = raw / scale
            else:
                extended[pl.ds(2 * clusters * side, clusters)] = halo_recv[side].astype(F32).reshape(
                    clusters, rhs, panels
                )

        def to_rows(p8, carry):
            for u in range(32):
                p = p8 * 32 + u
                x = extended[near_ids[1, p]].astype(BF16)
                terms[p] = dot_nt(x, nears[p])
            return carry

        lax.fori_loop(0, pairs // 32, to_rows, 0)
        image = image + one_hot_sum(keys_ref[0:1, :], terms[...].reshape(pairs * rhs, panels), flat)
        if it == 0:
            exchange_far()
        for share in shares:
            share.wait_recv()
        has_before = jnp.where(me > 0, 1.0, 0.0)
        has_after = jnp.where(me < n - 1, 1.0, 0.0)
        image = image + part_recv[it, 0].astype(F32) * has_after + part_recv[it, 1].astype(F32) * has_before
        wait_bytes(message_recv.at[it, pl.ds(0, n - 1)], msg_rsem.at[it])

        def far_terms(t8, total):
            for u in range(16):
                t = t8 * 16 + u
                arrived = message_recv[it, t].astype(F32)
                coeff, lean = arrived[:rhs], arrived[rhs:]
                spread = jnp.concatenate(
                    [
                        jnp.concatenate(
                            [
                                jnp.where(id_recv[t] == c, lean, 0.0),
                                jnp.where(row_ids[t] == c, coeff, 0.0),
                            ],
                            axis=1,
                        )
                        for c in range(clusters)
                    ],
                    axis=0,
                ).astype(BF16)
                total = total + dot_nn(spread, factors[t])
            return total

        image = lax.fori_loop(0, n // 16, far_terms, image).reshape(clusters, rhs, panels)

        count = it + 1
        vectors = [basis[b] for b in range(count)]
        inner = [row_sum(v * image) for v in vectors]
        gram = [row_sum(vectors[b] * vectors[d]) for b in range(count) for d in range(b, count)]
        diagonal = [gram[0]] if it == 0 else [gram[0], gram[2]]
        near_rest = image
        guesses = []
        for b in range(count):
            product = inner[0] if b == 0 else row_sum(vectors[b] * near_rest)
            wide = diagonal[b] > TINY
            guess = jnp.where(wide, product / jnp.where(wide, diagonal[b], 1.0), 0.0)
            near_rest = near_rest - guess[None] * vectors[b]
            guesses.append(guess)
        left_over = [row_sum(v * near_rest) for v in vectors]
        columns = inner + guesses + left_over + gram + [row_sum(near_rest * near_rest)]
        send_stats(1 + it, columns)
        got = get_stats(1 + it, len(columns))
        rows = [mean(got[b]) for b in range(count)]
        change = [rows[b] - got[count + b] for b in range(count)]
        square = got[-1]
        for b in range(count):
            square = square - 2.0 * change[b] * got[2 * count + b]
        place = 3 * count
        for b in range(count):
            for d in range(b, count):
                square = square + (1.0 if b == d else 2.0) * change[b] * change[d] * got[place]
                place += 1
        norm = jnp.sqrt(jnp.maximum(mean(square), 0.0) + epsilon)
        rest = image
        for b in range(count):
            rest = rest - to_column(rows[b])[None] * vectors[b]
        heights.extend(rows)
        heights.append(norm)
        following = rest / to_column(norm)[None]
        if it == 0:
            basis[1] = following
        else:
            for c in range(clusters):
                out_ref[:, c * panels:(c + 1) * panels] = following[c]

    for place, height in enumerate(heights):
        hess_ref[place:place + 1, :] = height[:, :rhs]

    for index in range(REDUCTIONS):
        wait_bytes(stat_recv.at[index, pl.ds(0, n - 1)], stat_ssem.at[index])
    wait_bytes(factors.at[pl.ds(0, n - 1), pl.ds(0, used)], fact_ssem.at[0])
    wait_bytes(id_recv.at[pl.ds(0, n - 1)], id_ssem.at[0])
    for side in range(2):
        wait_bytes(start_ref, raw_ssem.at[side])
        wait_bytes(halo_send, halo_ssem.at[side])
    for it in range(2):
        for side in range(2):
            wait_bytes(part_send.at[it, side], part_ssem.at[it, side])
        wait_bytes(message_recv.at[it, pl.ds(0, n - 1)], msg_ssem.at[it])


def per_device(start, self_blocks, near_pairs, near_blocks, far_pairs, far_left, far_right):
    n = lax.axis_size("dev")
    me = lax.axis_index("dev")
    rhs, width = start.shape
    clusters, panels, _ = self_blocks.shape
    pairs = near_pairs.shape[1]
    far_count = far_pairs.shape[1]
    rank = far_left.shape[1]
    most = max(2, 2 * far_count // n)
    used = most * rank
    flat = clusters * rhs
    near_rows = near_pairs[0] - me * clusters
    near_cols = near_pairs[1] - (me - 1) * clusters
    near_ids = jnp.stack([near_rows, near_cols])
    keys = (near_ids[:, :, None] * rhs + jnp.arange(rhs, dtype=jnp.int32)).reshape(2, pairs * rhs)
    target = far_pairs[1] // clusters
    order = jnp.arange(far_count, dtype=jnp.int32)
    earlier = (target[:, None] == target[None, :]) & (order[None, :] < order[:, None])
    slot = target * most + jnp.sum(earlier.astype(jnp.int32), axis=1)
    hit = slot[None, :] == jnp.arange(n * most, dtype=jnp.int32)[:, None]
    code = order * (clusters * clusters) + (far_pairs[0] - me * clusters) * clusters + far_pairs[1] % clusters
    code = jnp.sum(jnp.where(hit, code[None, :] + 1, 0), axis=1) - 1
    filled = code >= 0
    perm = jnp.where(filled, code // (clusters * clusters), 0)

    def spread(ids):
        ids = jnp.where(filled, ids, -1).reshape(n, most, 1)
        ids = jnp.broadcast_to(ids, (n, most, rank)).reshape(n, 1, used)
        ids = jnp.pad(ids, ((0, 0), (0, 0), (0, LANES - used)), constant_values=-1)
        return jnp.broadcast_to(ids, (n, rhs, LANES))

    row_ids = spread(code // clusters % clusters)
    col_ids = spread(code % clusters)
    smem = pl.BlockSpec(memory_space=pltpu.SMEM)
    vmem = pl.BlockSpec(memory_space=pltpu.VMEM)
    hbm = pl.BlockSpec(memory_space=pl.ANY)
    dma = pltpu.SemaphoreType.DMA
    return pl.pallas_call(
        functools.partial(kernel, n, most, float(width * n)),
        out_shape=(
            jax.ShapeDtypeStruct((rhs, width), F32),
            jax.ShapeDtypeStruct((5, rhs), F32),
        ),
        in_specs=[smem, smem, vmem, vmem, vmem, vmem, hbm, hbm, hbm, hbm],
        out_specs=(vmem, vmem),
        scratch_shapes=[
            pltpu.VMEM(self_blocks.shape, BF16),
            pltpu.VMEM(near_blocks.shape, BF16),
            pltpu.VMEM(far_left.shape, BF16),
            pltpu.VMEM(far_right.shape, BF16),
            pltpu.VMEM((n, 2 * LANES, panels), BF16),
            pltpu.VMEM((n, used, panels), BF16),
            pltpu.VMEM((n, rhs, LANES), jnp.int32),
            pltpu.VMEM((REDUCTIONS, STATS, LANES), F32),
            pltpu.VMEM((REDUCTIONS, n, STATS, LANES), F32),
            pltpu.VMEM((2, rhs, width), F32),
            pltpu.VMEM((flat, panels), BF16),
            pltpu.VMEM((2, flat, panels), BF16),
            pltpu.VMEM((2, 2, flat, panels), BF16),
            pltpu.VMEM((2, 2, flat, panels), BF16),
            pltpu.VMEM((2, n, 2 * rhs, LANES), BF16),
            pltpu.VMEM((2, n, 2 * rhs, LANES), BF16),
            pltpu.VMEM((3 * clusters, rhs, panels), F32),
            pltpu.VMEM((pairs, rhs, panels), F32),
            pltpu.VMEM((2, clusters, rhs, panels), F32),
            dma((3 + NEAR_CHUNKS,)),
            dma((2,)), dma((2,)),
            dma((REDUCTIONS,)),
            dma((REDUCTIONS,)),
            dma((1,)), dma((1,)), dma((1,)), dma((1,)),
            dma((2,)), dma((2,)), dma((2, 2)), dma((2, 2)),
            dma((2,)), dma((2,)),
        ],
        compiler_params=pltpu.CompilerParams(
            collective_id=0, has_side_effects=True, vmem_limit_bytes=60 * 1024 * 1024
        ),
    )(near_ids, perm, start, keys, row_ids, col_ids, self_blocks, near_blocks, far_left, far_right)


def solution(mesh):
    in_specs = (
        P(None, "dev"),
        P("dev", None, None),
        P(None, "dev"),
        P("dev", None, None),
        P(None, "dev"),
        P("dev", None, None),
        P("dev", None, None),
    )
    out_specs = (P(None, "dev"), P())
    return jax.shard_map(
        per_device, mesh=mesh, in_specs=in_specs, out_specs=out_specs, check_vma=False
    )
```
